256 devices in a mesh: dp: 256 (over z, y, x, core).
Axes of the slice: x: 4, y: 4, z: 8, core: 2. Of those that a mesh axis runs over, the one named last changes fastest.
Arguments:
- activations: bfloat16 [32768, 8192], P('dp'), may hold values from -6 to 6
- cotangent: bfloat16 [32768, 2048], P('dp'), may hold values from -0.5 to 0.5
- kept_tiles: int32 [256, 8], replicated, may hold values from 0 to 1023, as said below
- kept_counts: int32 [256], replicated, may hold values from 1 to 8
- chosen: int32 [256], replicated, may hold values from 0 to 1023, as said below
Outputs:
- summed_tiles: bfloat16 [256, 128, 128], replicated
The draws below stay inside these ranges and needn't reach their ends.
Inputs may be any that keep to these rules, and one draw needn't show every extreme that they name: `kept_tiles`: the 8 ids of one row lie in 8 different regions, where region of tile t is t // (1024 / 256); entries past the row's count are padding and name tiles too. `chosen`: entry q is a tile of region q.
All inputs are finite; a program needn't handle non-finite values.
Results may differ from the reference program's by a relative error of at most 0.001.
Values may be sent and summed in bfloat16 or wider, within the bound.
No kernel may reach another device: no remote copies, remote signals or barrier semaphores. Data moves between devices by JAX's collectives and lax.ppermute only.
A program may use at most 128 MiB of HBM per device.

```python
import jax
import jax.numpy as jnp
from jax import lax

FF_WIN = 8192
D_WIN = 2048
TILE = 128
KEPT = 8
TOK_DEV = 128
TOKENS = 32768
TILES = 1024
N_DP = 256


def chosen_offsets(key):
    return jax.random.randint(jax.random.fold_in(key, 11), (N_DP,), 0, TILES // N_DP)


def draw_chosen(key, part):
    offsets = chosen_offsets(key)
    return (jnp.arange(N_DP, dtype=jnp.int32) * (TILES // N_DP) + offsets).astype(jnp.int32)


def draw_kept_tiles(key, part):
    offsets = chosen_offsets(key)
    key = jax.random.fold_in(key, 3)
    key_region, key_coin, key_other = jax.random.split(key, 3)
    region_keys = jax.random.split(key_region, N_DP)
    regions = jax.vmap(lambda small_key: jax.random.permutation(small_key, N_DP)[:KEPT])(region_keys)
    coins = jax.random.randint(key_coin, (N_DP, KEPT), 0, 2)
    others = jax.random.randint(key_other, (N_DP, KEPT), 0, TILES // N_DP)
    picked = jnp.where(coins == 1, offsets[regions], others)
    return (regions * (TILES // N_DP) + picked).astype(jnp.int32)


def draw_kept_counts(key, part):
    key = jax.random.fold_in(key, 5)
    key_count, key_place = jax.random.split(key)
    counts = jax.random.randint(key_count, (N_DP,), 1, KEPT + 1)
    place = jax.random.randint(key_place, (), 0, N_DP)
    return counts.at[place].set(KEPT).astype(jnp.int32)


def steps_of(own_key, shape, cuts, smallest, high):
    def one(position, blocks):
        steps = jax.random.uniform(jax.random.fold_in(jax.random.fold_in(own_key, 6), position), (blocks,), jnp.float32, smallest / len(cuts), high / len(cuts))
        return jnp.repeat(jnp.exp(steps), shape[position] // blocks).reshape((-1,) + (1,) * (len(shape) - position - 1))

    level = one(*cuts[0])
    for cut in cuts[1:]:
        level = level * one(*cut)
    return level


def normal_values(rng, shape, spread, most, pieces=(), kind=jnp.bfloat16):
    entries = jax.random.normal(rng, shape, jnp.float32) * spread
    if len(pieces) > 0:
        entries = steps_of(rng, shape, pieces, -0.22, 0.18) * entries
    return jnp.clip(entries, min=-most, max=most).astype(kind)


def setup_inputs(seed: int = 0) -> dict:
    seeds = jax.random.split(jax.random.key(seed), 6)
    activations = normal_values(seeds[0], (TOKENS, FF_WIN), 1.0, 6.0, ((0, 256),))
    cotangent = normal_values(seeds[1], (TOKENS, D_WIN), TOK_DEV ** -0.5, 0.5, ((0, 256),))
    kept_tiles = draw_kept_tiles(jax.random.fold_in(seeds[5], 71), 0)
    kept_counts = draw_kept_counts(jax.random.fold_in(seeds[5], 71), 0)
    chosen = draw_chosen(jax.random.fold_in(seeds[5], 71), 0)
    return {"activations": activations, "cotangent": cotangent, "kept_tiles": kept_tiles, "kept_counts": kept_counts, "chosen": chosen}


def reference(activations, cotangent, kept_tiles, kept_counts, chosen):
    col_blocks = D_WIN // TILE
    acts = activations.reshape(N_DP, TOK_DEV, FF_WIN // TILE, TILE)
    cots = cotangent.reshape(N_DP, TOK_DEV, col_blocks, TILE)

    def one_replica(carry, inputs):
        act_blocks, cot_blocks, tile_ids, count = inputs
        left = jnp.take(act_blocks, (tile_ids // col_blocks).astype(jnp.int32), axis=1).astype(jnp.float32)
        right = jnp.take(cot_blocks, (tile_ids % col_blocks).astype(jnp.int32), axis=1).astype(jnp.float32)
        tiles = jnp.einsum("skr,skc->krc", left, right, precision=lax.Precision.HIGHEST)
        live = jnp.arange(KEPT, dtype=jnp.int32) < count
        match = ((chosen[:, None] == tile_ids[None, :]) & live[None, :]).astype(jnp.float32)
        terms = jnp.dot(match, tiles.reshape(KEPT, TILE * TILE), precision=lax.Precision.HIGHEST)
        return carry + terms, None

    start = jnp.zeros((N_DP, TILE * TILE), jnp.float32)
    total, unused = lax.scan(one_replica, start, (acts, cots, kept_tiles, kept_counts))
    return total.reshape(N_DP, TILE, TILE).astype(jnp.bfloat16)
```

```python
import jax
import jax.numpy as jnp
from jax import lax
from jax.experimental import pallas as pl
from jax.experimental.pallas import tpu as pltpu
from jax.sharding import PartitionSpec as P

TILE = 128
KEPT = 8
N_DP = 256
COLS = 16
ZN, YN, XN, CN = 8, 4, 4, 2
CHIPS = 128
HALF = 128
HALF_TILES = 512
VMEM_LIMIT = 48 * 1024 * 1024


def dev(z, y, x, c):
    return ((z * YN + y) * XN + x) * CN + c


DEVS = [(z, y, x, c) for z in range(ZN) for y in range(YN) for x in range(XN) for c in range(CN)]
CHIP_GROUPS = [[chip * CN + c for chip in range(CHIPS)] for c in range(CN)]
Z_GROUPS = [[dev(z, y, x, c) for z in range(ZN)] for y in range(YN) for x in range(XN) for c in range(CN)]
SWAP = [(d, d ^ 1) for d in range(N_DP)]


def ring(step, turn):
    pairs = []
    for z, y, x, c in DEVS:
        if (c + turn) % 2 == 0:
            pairs.append((dev(z, y, x, c), dev(z, (y + step) % YN, x, c)))
        else:
            pairs.append((dev(z, y, x, c), dev(z, y, (x + step) % XN, c)))
    return pairs


def tiles_kernel(ids_ref, act_ref, cot_ref, out_ref, lefts, rights, stage, sems):
    copies = []
    for k in range(KEPT):
        tile = ids_ref[k]
        row = pl.multiple_of((tile // COLS) * TILE, TILE)
        col = pl.multiple_of((tile % COLS) * TILE, TILE)
        a = pltpu.make_async_copy(act_ref.at[:, pl.ds(row, TILE)], lefts.at[k], sems.at[k, 0])
        b = pltpu.make_async_copy(cot_ref.at[:, pl.ds(col, TILE)], rights.at[k], sems.at[k, 1])
        a.start()
        b.start()
        copies.append((a, b))
    for k in range(KEPT):
        a, b = copies[k]
        a.wait()
        b.wait()
        half = ids_ref[k] // HALF_TILES
        tile = lax.dot_general(
            lefts[k], rights[k], (((0,), (0,)), ((), ())), preferred_element_type=jnp.float32
        )
        for p in range(4):
            for q in range(4):
                there = jnp.where(half == 0, p * 32 + q * 8, q * 32 + p * 8) + k * TILE
                here = p * 32 + q * 8
                stage[pl.ds(pl.multiple_of(there, 8), 8), :] = tile[here:here + 8, :]
    for chip in range(CHIPS):
        z, y, x = chip // 16, (chip // 4) % 4, chip % 4
        out_ref[chip] = stage[pl.ds(x * 32 + y * 8 + z, KEPT, stride=TILE), :]


def own_tiles(ids, activations, cotangent):
    return pl.pallas_call(
        tiles_kernel,
        out_shape=jax.ShapeDtypeStruct((CHIPS, KEPT, TILE), jnp.float32),
        in_specs=[
            pl.BlockSpec(memory_space=pltpu.SMEM),
            pl.BlockSpec(memory_space=pl.ANY),
            pl.BlockSpec(memory_space=pl.ANY),
        ],
        out_specs=pl.BlockSpec(memory_space=pltpu.VMEM),
        scratch_shapes=[
            pltpu.VMEM((KEPT, TILE, TILE), jnp.bfloat16),
            pltpu.VMEM((KEPT, TILE, TILE), jnp.bfloat16),
            pltpu.VMEM((KEPT * TILE, TILE), jnp.float32),
            pltpu.SemaphoreType.DMA((KEPT, 2)),
        ],
        compiler_params=pltpu.CompilerParams(vmem_limit_bytes=VMEM_LIMIT),
        name="own_tiles",
    )(ids, activations, cotangent)


def rows_kernel(place_ref, p0, p1, p2, p3, out_ref, wide):
    for step, piece in enumerate((p0, p1, p2, p3)):
        slot = place_ref[step]
        wide[pl.ds(pl.multiple_of(slot * ZN * HALF, ZN * HALF), ZN * HALF), :] = (
            piece[...].astype(jnp.float32).reshape(ZN * HALF, TILE)
        )

    def body(t, carry):
        rows = [wide[pl.ds(q * ZN * HALF + t, ZN, stride=HALF), :] for q in range(4)]
        out_ref[t] = jnp.concatenate(rows, axis=0).astype(jnp.bfloat16)
        return carry

    lax.fori_loop(0, HALF, body, 0, unroll=8)


def by_rows(place, pieces):
    return pl.pallas_call(
        rows_kernel,
        out_shape=jax.ShapeDtypeStruct((HALF, 4 * ZN, TILE), jnp.bfloat16),
        in_specs=[pl.BlockSpec(memory_space=pltpu.SMEM)] + [pl.BlockSpec(memory_space=pltpu.VMEM)] * 4,
        out_specs=pl.BlockSpec(memory_space=pltpu.VMEM),
        scratch_shapes=[pltpu.VMEM((4 * ZN * HALF, TILE), jnp.float32)],
        compiler_params=pltpu.CompilerParams(vmem_limit_bytes=VMEM_LIMIT),
        name="by_rows",
    )(place, *pieces)


def join_kernel(place_ref, *refs):
    pieces, out_ref, sems = refs[:8], refs[8], refs[9]
    copies = []
    for i, piece in enumerate(pieces):
        half = place_ref[8 + i]
        slot = place_ref[i]
        copies.append(pltpu.make_async_copy(
            piece, out_ref.at[pl.ds(pl.multiple_of(half * HALF, HALF), HALF), slot], sems.at[i]
        ))
    for copy in copies:
        copy.start()
    for copy in copies:
        copy.wait()


def join(place, pieces):
    return pl.pallas_call(
        join_kernel,
        out_shape=jax.ShapeDtypeStruct((N_DP, 4, 32, TILE), jnp.bfloat16),
        in_specs=[pl.BlockSpec(memory_space=pltpu.SMEM)] + [pl.BlockSpec(memory_space=pl.ANY)] * 8,
        out_specs=pl.BlockSpec(memory_space=pl.ANY),
        scratch_shapes=[pltpu.SemaphoreType.DMA((8,))],
        name="join",
    )(place, *pieces)


def local(activations, cotangent, kept_tiles, kept_counts, chosen):
    me = lax.axis_index("dp")
    core = me % CN
    x = (me // CN) % XN
    y = (me // (CN * XN)) % YN
    own_ids = lax.dynamic_index_in_dim(kept_tiles, me, 0, keepdims=False)
    sent = own_tiles(own_ids, activations, cotangent)
    got = lax.all_to_all(sent, "dp", 0, 0, axis_index_groups=CHIP_GROUPS, tiled=True)

    live = jnp.arange(KEPT, dtype=jnp.int32)[None, :] < kept_counts[:, None]
    ids = jnp.where(live, kept_tiles, -1).reshape(CHIPS, CN, KEPT)
    ids = lax.dynamic_index_in_dim(ids, core, 1, keepdims=False).reshape(CHIPS * KEPT)
    match = (chosen[:, None] == ids[None, :]).astype(jnp.float32)
    part = jnp.dot(match, got.reshape(CHIPS * KEPT, TILE), precision=lax.Precision.HIGHEST)
    part = part.reshape(CN, HALF, TILE)
    mine = lax.dynamic_index_in_dim(part, core, 0, keepdims=False)
    theirs = lax.dynamic_index_in_dim(part, 1 - core, 0, keepdims=False)
    row = (mine + lax.ppermute(theirs, "dp", SWAP)).astype(jnp.bfloat16)

    rows = lax.all_to_all(
        jnp.broadcast_to(row[None], (ZN, HALF, TILE)), "dp", 0, 0, axis_index_groups=Z_GROUPS, tiled=True
    )
    steps = (0, 1, 3, 2)
    at0 = jnp.where(core == 0, y, x)
    at1 = jnp.where(core == 0, x, y)
    pieces = [rows] + [lax.ppermute(rows, "dp", ring(s, 0)) for s in steps[1:]]
    block = by_rows(jnp.stack([(at0 - s) % 4 for s in steps]), pieces)
    blocks = [block] + [lax.ppermute(block, "dp", ring(s, 1)) for s in steps[1:]]
    other = [lax.ppermute(b, "dp", SWAP) for b in blocks]
    place = jnp.stack(
        [(at1 - s) % 4 for s in steps] + [(at0 - s) % 4 for s in steps] + [core] * 4 + [1 - core] * 4
    )
    return join(place, blocks + other).reshape(N_DP, TILE, TILE)


def solution(mesh):
    return jax.shard_map(
        local,
        mesh=mesh,
        in_specs=(P("dp", None), P("dp", None), P(), P(), P()),
        out_specs=P(),
        check_vma=False,
    )
```

```python
import jax
import jax.numpy as jnp
from jax import lax
from jax.experimental import pallas as pl
from jax.experimental.pallas import tpu as pltpu
from jax.sharding import PartitionSpec as P

TILE = 128
KEPT = 8
N_DP = 256
COLS = 16
ZN, YN, XN, CN = 8, 4, 4, 2
CHIPS = 128
HALF = 128
HALF_TILES = 512
JOIN = 16
VMEM_LIMIT = 48 * 1024 * 1024


def dev(z, y, x, c):
    return ((z * YN + y) * XN + x) * CN + c


DEVS = [(z, y, x, c) for z in range(ZN) for y in range(YN) for x in range(XN) for c in range(CN)]
CHIP_GROUPS = [[chip * CN + c for chip in range(CHIPS)] for c in range(CN)]
Z_GROUPS = [[dev(z, y, x, c) for z in range(ZN)] for y in range(YN) for x in range(XN) for c in range(CN)]
SWAP = [(d, d ^ 1) for d in range(N_DP)]


def ring(step, turn):
    pairs = []
    for z, y, x, c in DEVS:
        if (c + turn) % 2 == 0:
            pairs.append((dev(z, y, x, c), dev(z, (y + step) % YN, x, c)))
        else:
            pairs.append((dev(z, y, x, c), dev(z, y, (x + step) % XN, c)))
    return pairs


def tiles_kernel(ids_ref, act_ref, cot_ref, out_ref, lefts, rights, stage, sems):
    copies = []
    for k in range(KEPT):
        tile = ids_ref[k]
        row = pl.multiple_of((tile // COLS) * TILE, TILE)
        col = pl.multiple_of((tile % COLS) * TILE, TILE)
        a = pltpu.make_async_copy(act_ref.at[:, pl.ds(row, TILE)], lefts.at[k], sems.at[k, 0])
        b = pltpu.make_async_copy(cot_ref.at[:, pl.ds(col, TILE)], rights.at[k], sems.at[k, 1])
        a.start()
        b.start()
        copies.append((a, b))
    for k in range(KEPT):
        a, b = copies[k]
        a.wait()
        b.wait()
        half = ids_ref[k] // HALF_TILES
        tile = lax.dot_general(
            lefts[k], rights[k], (((0,), (0,)), ((), ())), preferred_element_type=jnp.float32
        )
        for p in range(4):
            for q in range(4):
                there = jnp.where(half == 0, p * 32 + q * 8, q * 32 + p * 8) + k * TILE
                here = p * 32 + q * 8
                stage[pl.ds(pl.multiple_of(there, 8), 8), :] = tile[here:here + 8, :]
    for chip in range(CHIPS):
        z, y, x = chip // 16, (chip // 4) % 4, chip % 4
        out_ref[chip] = stage[pl.ds(x * 32 + y * 8 + z, KEPT, stride=TILE), :]


def own_tiles(ids, activations, cotangent):
    return pl.pallas_call(
        tiles_kernel,
        out_shape=jax.ShapeDtypeStruct((CHIPS, KEPT, TILE), jnp.float32),
        in_specs=[
            pl.BlockSpec(memory_space=pltpu.SMEM),
            pl.BlockSpec(memory_space=pl.ANY),
            pl.BlockSpec(memory_space=pl.ANY),
        ],
        out_specs=pl.BlockSpec(memory_space=pltpu.VMEM),
        scratch_shapes=[
            pltpu.VMEM((KEPT, TILE, TILE), jnp.bfloat16),
            pltpu.VMEM((KEPT, TILE, TILE), jnp.bfloat16),
            pltpu.VMEM((KEPT * TILE, TILE), jnp.float32),
            pltpu.SemaphoreType.DMA((KEPT, 2)),
        ],
        compiler_params=pltpu.CompilerParams(vmem_limit_bytes=VMEM_LIMIT),
        name="own_tiles",
    )(ids, activations, cotangent)


def rows_kernel(place_ref, p0, p1, p2, p3, out_ref, wide):
    for step, piece in enumerate((p0, p1, p2, p3)):
        slot = place_ref[step]
        wide[pl.ds(pl.multiple_of(slot * ZN * HALF, ZN * HALF), ZN * HALF), :] = (
            piece[...].astype(jnp.float32).reshape(ZN * HALF, TILE)
        )

    def body(t, carry):
        rows = [wide[pl.ds(q * ZN * HALF + t, ZN, stride=HALF), :] for q in range(4)]
        out_ref[t] = jnp.concatenate(rows, axis=0).astype(jnp.bfloat16)
        return carry

    lax.fori_loop(0, HALF, body, 0, unroll=8)


def by_rows(place, pieces):
    return pl.pallas_call(
        rows_kernel,
        out_shape=jax.ShapeDtypeStruct((HALF, 4 * ZN, TILE), jnp.bfloat16),
        in_specs=[pl.BlockSpec(memory_space=pltpu.SMEM)] + [pl.BlockSpec(memory_space=pltpu.VMEM)] * 4,
        out_specs=pl.BlockSpec(memory_space=pltpu.VMEM),
        scratch_shapes=[pltpu.VMEM((4 * ZN * HALF, TILE), jnp.float32)],
        compiler_params=pltpu.CompilerParams(vmem_limit_bytes=VMEM_LIMIT),
        name="by_rows",
    )(place, *pieces)


def join_kernel(place_ref, *refs):
    pieces, out_ref = refs[:8], refs[8]
    rows = pl.ds(pl.program_id(1) * JOIN, JOIN)
    for g in range(2):
        @pl.when(pl.program_id(0) == g)
        def _():
            for j in range(4 * g, 4 * g + 4):
                out_ref[0, :, place_ref[j]] = pieces[j][rows]


def join(place, pieces):
    return pl.pallas_call(
        join_kernel,
        grid_spec=pltpu.PrefetchScalarGridSpec(
            num_scalar_prefetch=1,
            grid=(2, HALF // JOIN),
            in_specs=[pl.BlockSpec(memory_space=pltpu.VMEM)] * 8,
            out_specs=pl.BlockSpec((1, JOIN, 4, 32, TILE), lambda g, i, place: (place[8 + g], i, 0, 0, 0)),
        ),
        out_shape=jax.ShapeDtypeStruct((2, HALF, 4, 32, TILE), jnp.bfloat16),
        compiler_params=pltpu.CompilerParams(vmem_limit_bytes=VMEM_LIMIT),
        name="join",
    )(place, *pieces)


def local(activations, cotangent, kept_tiles, kept_counts, chosen):
    me = lax.axis_index("dp")
    core = me % CN
    x = (me // CN) % XN
    y = (me // (CN * XN)) % YN
    own_ids = lax.dynamic_index_in_dim(kept_tiles, me, 0, keepdims=False)
    sent = own_tiles(own_ids, activations, cotangent)
    got = lax.all_to_all(sent, "dp", 0, 0, axis_index_groups=CHIP_GROUPS, tiled=True)

    live = jnp.arange(KEPT, dtype=jnp.int32)[None, :] < kept_counts[:, None]
    ids = jnp.where(live, kept_tiles, -1).reshape(CHIPS, CN, KEPT)
    ids = lax.dynamic_index_in_dim(ids, core, 1, keepdims=False).reshape(CHIPS * KEPT)
    match = (chosen[:, None] == ids[None, :]).astype(jnp.float32)
    part = jnp.dot(match, got.reshape(CHIPS * KEPT, TILE), precision=lax.Precision.HIGHEST)
    part = part.reshape(CN, HALF, TILE)
    mine = lax.dynamic_index_in_dim(part, core, 0, keepdims=False)
    theirs = lax.dynamic_index_in_dim(part, 1 - core, 0, keepdims=False)
    row = (mine + lax.ppermute(theirs, "dp", SWAP)).astype(jnp.bfloat16)

    rows = lax.all_to_all(
        jnp.broadcast_to(row[None], (ZN, HALF, TILE)), "dp", 0, 0, axis_index_groups=Z_GROUPS, tiled=True
    )
    steps = (0, 1, 3, 2)
    at0 = jnp.where(core == 0, y, x)
    at1 = jnp.where(core == 0, x, y)
    pieces = [rows] + [lax.ppermute(rows, "dp", ring(s, 0)) for s in steps[1:]]
    block = by_rows(jnp.stack([(at0 - s) % 4 for s in steps]), pieces)
    blocks = [block] + [lax.ppermute(block, "dp", ring(s, 1)) for s in steps[1:]]
    other = [lax.ppermute(b, "dp", SWAP) for b in blocks]
    place = jnp.stack(
        [(at1 - s) % 4 for s in steps] + [(at0 - s) % 4 for s in steps] + [core, 1 - core]
    )
    return join(place, blocks + other).reshape(N_DP, TILE, TILE)


def solution(mesh):
    return jax.shard_map(
        local,
        mesh=mesh,
        in_specs=(P("dp", None), P("dp", None), P(), P(), P()),
        out_specs=P(),
        check_vma=False,
    )
```

```python
import functools

import jax
import jax.numpy as jnp
from jax import lax
from jax.experimental import pallas as pl
from jax.experimental.pallas import tpu as pltpu
from jax.sharding import PartitionSpec as P

TILE = 128
KEPT = 8
N_DP = 256
COLS = 16
ZN, YN, XN, CN = 8, 4, 4, 2
CHIPS = 128
HALF = 128
HALF_TILES = 512
MIB = 1024 * 1024
PART = 64
STEPS = (0, 1, 3, 2)


def dev(z, y, x, c):
    return ((z * YN + y) * XN + x) * CN + c


DEVS = [(z, y, x, c) for z in range(ZN) for y in range(YN) for x in range(XN) for c in range(CN)]
CHIP_GROUPS = [[dev(z, y, x, c) for x in range(XN) for y in range(YN) for z in range(ZN)] for c in range(CN)]
Z_GROUPS = [[dev(z, y, x, c) for z in range(ZN)] for y in range(YN) for x in range(XN) for c in range(CN)]
SWAP = [(d, d ^ 1) for d in range(N_DP)]


def ring(step, turn):
    pairs = []
    for z, y, x, c in DEVS:
        if (c + turn) % 2 == 0:
            pairs.append((dev(z, y, x, c), dev(z, (y + step) % YN, x, c)))
        else:
            pairs.append((dev(z, y, x, c), dev(z, y, (x + step) % XN, c)))
    return pairs


def spot():
    me = lax.axis_index("dp")
    core = me % CN
    x = (me // CN) % XN
    y = (me // (CN * XN)) % YN
    return core, jnp.where(core == 0, y, x), jnp.where(core == 0, x, y)


def tiles_kernel(kept_ref, act_ref, cot_ref, out_ref, lefts, rights, stage, sems):
    me = lax.axis_index("dp")
    copies = []
    for k in range(KEPT):
        tile = kept_ref[k, me]
        row = pl.multiple_of((tile // COLS) * TILE, TILE)
        col = pl.multiple_of((tile % COLS) * TILE, TILE)
        a = pltpu.make_async_copy(act_ref.at[:, pl.ds(row, TILE)], lefts.at[k], sems.at[k, 0])
        b = pltpu.make_async_copy(cot_ref.at[:, pl.ds(col, TILE)], rights.at[k], sems.at[k, 1])
        a.start()
        b.start()
        copies.append((a, b))
    for k in range(KEPT):
        a, b = copies[k]
        a.wait()
        b.wait()
        half = kept_ref[k, me] // HALF_TILES
        tile = lax.dot_general(
            lefts[k], rights[k], (((0,), (0,)), ((), ())), preferred_element_type=jnp.float32
        )
        for p in range(4):
            for q in range(4):
                there = jnp.where(half == 0, p * 32 + q * 8, q * 32 + p * 8) + k * TILE
                here = p * 32 + q * 8
                stage[pl.ds(pl.multiple_of(there, 8), 8), :] = tile[here:here + 8, :]
    for chip in range(CHIPS):
        out_ref[chip] = stage[pl.ds(chip, KEPT, stride=TILE), :]


def own_tiles(kept, activations, cotangent):
    return pl.pallas_call(
        tiles_kernel,
        out_shape=jax.ShapeDtypeStruct((CHIPS, KEPT, TILE), jnp.float32),
        in_specs=[
            pl.BlockSpec(memory_space=pltpu.SMEM),
            pl.BlockSpec(memory_space=pltpu.HBM),
            pl.BlockSpec(memory_space=pltpu.HBM),
        ],
        out_specs=pl.BlockSpec(memory_space=pltpu.VMEM),
        scratch_shapes=[
            pltpu.VMEM((KEPT, TILE, TILE), jnp.bfloat16),
            pltpu.VMEM((KEPT, TILE, TILE), jnp.bfloat16),
            pltpu.VMEM((KEPT * TILE, TILE), jnp.float32),
            pltpu.SemaphoreType.DMA((KEPT, 2)),
        ],
        compiler_params=pltpu.CompilerParams(vmem_limit_bytes=62 * MIB),
        name="own_tiles",
    )(kept, activations, cotangent)


def rows_kernel(p0, p1, p2, p3, a_ref, b_ref, wide):
    at = spot()[1]
    for step, piece in zip(STEPS, (p0, p1, p2, p3)):
        start = pl.multiple_of((at + 4 - step) % 4 * ZN * HALF, ZN * HALF)
        wide[pl.ds(start, ZN * HALF), :] = piece[...].astype(jnp.float32).reshape(ZN * HALF, TILE)

    for part, out_ref in enumerate((a_ref, b_ref)):
        def body(t, carry):
            rows = [wide[pl.ds(q * ZN * HALF + part * PART + t, ZN, stride=HALF), :] for q in range(4)]
            out_ref[t] = jnp.concatenate(rows, axis=0).astype(jnp.bfloat16)
            return carry

        lax.fori_loop(0, PART, body, 0, unroll=8)


def by_rows(pieces):
    return pl.pallas_call(
        rows_kernel,
        out_shape=[jax.ShapeDtypeStruct((PART, 4 * ZN, TILE), jnp.bfloat16)] * 2,
        in_specs=[pl.BlockSpec(memory_space=pltpu.VMEM)] * 4,
        out_specs=[pl.BlockSpec(memory_space=pltpu.VMEM)] * 2,
        scratch_shapes=[pltpu.VMEM((4 * ZN * HALF, TILE), jnp.float32)],
        compiler_params=pltpu.CompilerParams(vmem_limit_bytes=8 * MIB),
        name="by_rows",
    )(*pieces)


def join_kernel(spots, *refs):
    out_ref, sems = refs[-2], refs[-1]
    core, at0, at1 = spot()
    copies = []
    for i, (other, part, step) in enumerate(spots):
        half, at = (1 - core, at0) if other else (core, at1)
        copies.append(pltpu.make_async_copy(refs[i], out_ref.at[half, part, :, (at + 4 - step) % 4], sems.at[i]))
    for copy in copies:
        copy.start()
    for copy in copies:
        copy.wait()


def join(spots, pieces, out=None):
    n = len(spots)
    more = [] if out is None else [out]
    size = n * PART * 32 * TILE * 2
    return pl.pallas_call(
        functools.partial(join_kernel, spots),
        out_shape=jax.ShapeDtypeStruct((2, 2, PART, 4, 32, TILE), jnp.bfloat16),
        in_specs=[pl.BlockSpec(memory_space=pltpu.VMEM)] * n + [pl.BlockSpec(memory_space=pltpu.HBM)] * len(more),
        out_specs=pl.BlockSpec(memory_space=pltpu.HBM),
        scratch_shapes=[pltpu.SemaphoreType.DMA((n,))],
        input_output_aliases={} if out is None else {n: 0},
        compiler_params=pltpu.CompilerParams(vmem_limit_bytes=2 * MIB),
        cost_estimate=pl.CostEstimate(flops=0, bytes_accessed=2 * size, transcendentals=0),
        name="join",
    )(*pieces, *more)


def local(activations, cotangent, kept_tiles, kept_counts, chosen):
    me = lax.axis_index("dp")
    core = me % CN
    sent = own_tiles(kept_tiles.T, activations, cotangent)
    live = jnp.arange(KEPT, dtype=jnp.int32)[None, :] < kept_counts[:, None]
    ids = jnp.where(live, kept_tiles, -1).reshape(ZN, YN, XN, CN, KEPT)
    ids = lax.dynamic_index_in_dim(ids, core, 3, keepdims=False)
    ids = ids.transpose(2, 1, 0, 3).reshape(CHIPS * KEPT)
    got = lax.all_to_all(sent, "dp", 0, 0, axis_index_groups=CHIP_GROUPS, tiled=True)

    match = (chosen[:, None] == ids[None, :]).astype(jnp.float32)
    part = jnp.dot(match, got.reshape(CHIPS * KEPT, TILE), precision=lax.Precision.HIGHEST)
    part = part.reshape(CN, HALF, TILE)
    mine = lax.dynamic_index_in_dim(part, core, 0, keepdims=False)
    theirs = lax.dynamic_index_in_dim(part, 1 - core, 0, keepdims=False)
    row = (mine + lax.ppermute(theirs, "dp", SWAP)).astype(jnp.bfloat16)

    rows = lax.all_to_all(
        jnp.broadcast_to(row[None], (ZN, HALF, TILE)), "dp", 0, 0, axis_index_groups=Z_GROUPS, tiled=True
    )
    def swap(blocks):
        return [lax.ppermute(b, "dp", SWAP) for b in blocks]

    a0, b0 = by_rows([rows] + [lax.ppermute(rows, "dp", ring(s, 0)) for s in STEPS[1:]])
    a1 = lax.ppermute(a0, "dp", ring(1, 1))
    b3 = lax.ppermute(b0, "dp", ring(3, 1))
    b1 = lax.ppermute(b0, "dp", ring(1, 1))
    a3 = lax.ppermute(a0, "dp", ring(3, 1))
    a2 = lax.ppermute(a1, "dp", ring(1, 1))
    b2 = lax.ppermute(b3, "dp", ring(3, 1))
    out = None
    for steps, blocks in (
        ((0, 0), (a0, b0)),
        ((1, 3, 1, 3), (a1, a3, b1, b3)),
        ((2, 2), (a2, b2)),
    ):
        n = len(steps)
        spots = tuple((o, i * 2 // n, steps[i]) for o in range(2) for i in range(n))
        out = join(spots, list(blocks) + swap(blocks), out)
    return out.reshape(N_DP, TILE, TILE)


def solution(mesh):
    return jax.shard_map(
        local,
        mesh=mesh,
        in_specs=(P("dp", None), P("dp", None), P(), P(), P()),
        out_specs=P(),
        check_vma=False,
    )
```

```python
import functools

import jax
import jax.numpy as jnp
import numpy as np
from jax import lax
from jax.experimental import pallas as pl
from jax.experimental.pallas import tpu as pltpu
from jax.sharding import PartitionSpec as P

TILE = 128
KEPT = 8
N_DP = 256
COLS = 16
ZN, YN, XN, CN = 8, 4, 4, 2
CHIPS = 128
HALF = 128
HALF_TILES = 512
MIB = 1024 * 1024
PART = 64
STEPS = (0, 1, 3, 2)


def dev(z, y, x, c):
    return ((z * YN + y) * XN + x) * CN + c


DEVS = [(z, y, x, c) for z in range(ZN) for y in range(YN) for x in range(XN) for c in range(CN)]
CHIP_GROUPS = [[dev(z, y, x, c) for y in range(YN) for z in range(ZN) for x in range(XN)] for c in range(CN)]
Z_GROUPS = [[dev(z, y, x, c) for z in range(ZN)] for y in range(YN) for x in range(XN) for c in range(CN)]
SWAP = [(d, d ^ 1) for d in range(N_DP)]


def ring(step, turn):
    pairs = []
    for z, y, x, c in DEVS:
        if (c + turn) % 2 == 0:
            pairs.append((dev(z, y, x, c), dev(z, (y + step) % YN, x, c)))
        else:
            pairs.append((dev(z, y, x, c), dev(z, y, (x + step) % XN, c)))
    return pairs


def spot():
    me = lax.axis_index("dp")
    core = me % CN
    x = (me // CN) % XN
    y = (me // (CN * XN)) % YN
    return core, jnp.where(core == 0, y, x), jnp.where(core == 0, x, y)


def tiles_kernel(kept_ref, act_ref, cot_ref, out_ref, lefts, rights, stage, sems):
    me = lax.axis_index("dp")
    for k in range(KEPT):
        tile = kept_ref[k, me]
        row = pl.multiple_of((tile // COLS) * TILE, TILE)
        col = pl.multiple_of((tile % COLS) * TILE, TILE)
        pltpu.make_async_copy(act_ref.at[:, pl.ds(row, TILE)], lefts.at[k], sems.at[0]).start()
        pltpu.make_async_copy(cot_ref.at[:, pl.ds(col, TILE)], rights.at[k], sems.at[1]).start()
    pltpu.make_async_copy(lefts, lefts, sems.at[0]).wait()
    pltpu.make_async_copy(rights, rights, sems.at[1]).wait()
    for k in range(KEPT):
        half = kept_ref[k, me] // HALF_TILES
        tile = lax.dot_general(
            lefts[k], rights[k], (((0,), (0,)), ((), ())), preferred_element_type=jnp.float32
        )
        for p in range(4):
            for q in range(4):
                there = jnp.where(half == 0, p * 32 + q * 8, q * 32 + p * 8) + k * TILE
                here = p * 32 + q * 8
                stage[pl.ds(pl.multiple_of(there, 8), 8), :] = tile[here:here + 8, :]
    for i, (y, z, x) in enumerate(np.ndindex(YN, ZN, XN)):
        out_ref[i] = stage[pl.ds(x * 32 + y * 8 + z, KEPT, stride=TILE), :]


def own_tiles(kept, activations, cotangent):
    return pl.pallas_call(
        tiles_kernel,
        out_shape=jax.ShapeDtypeStruct((CHIPS, KEPT, TILE), jnp.float32),
        in_specs=[
            pl.BlockSpec(memory_space=pltpu.SMEM),
            pl.BlockSpec(memory_space=pltpu.HBM),
            pl.BlockSpec(memory_space=pltpu.HBM),
        ],
        out_specs=pl.BlockSpec(memory_space=pltpu.VMEM),
        scratch_shapes=[
            pltpu.VMEM((KEPT, TILE, TILE), jnp.bfloat16),
            pltpu.VMEM((KEPT, TILE, TILE), jnp.bfloat16),
            pltpu.VMEM((KEPT * TILE, TILE), jnp.float32),
            pltpu.SemaphoreType.DMA((2,)),
        ],
        compiler_params=pltpu.CompilerParams(vmem_limit_bytes=62 * MIB),
        name="own_tiles",
    )(kept, activations, cotangent)


def rows_kernel(p0, p1, p2, p3, a_ref, b_ref, wide):
    at = spot()[1]
    for step, piece in zip(STEPS, (p0, p1, p2, p3)):
        start = pl.multiple_of((at + 4 - step) % 4 * ZN * HALF, ZN * HALF)
        wide[pl.ds(start, ZN * HALF), :] = piece[...].astype(jnp.float32).reshape(ZN * HALF, TILE)

    for part, out_ref in enumerate((a_ref, b_ref)):
        def body(t, carry):
            rows = [wide[pl.ds(q * ZN * HALF + part * PART + t, ZN, stride=HALF), :] for q in range(4)]
            out_ref[t] = jnp.concatenate(rows, axis=0).astype(jnp.bfloat16)
            return carry

        lax.fori_loop(0, PART, body, 0, unroll=8)


def by_rows(pieces):
    return pl.pallas_call(
        rows_kernel,
        out_shape=[jax.ShapeDtypeStruct((PART, 4 * ZN, TILE), jnp.bfloat16)] * 2,
        in_specs=[pl.BlockSpec(memory_space=pltpu.VMEM)] * 4,
        out_specs=[pl.BlockSpec(memory_space=pltpu.VMEM)] * 2,
        scratch_shapes=[pltpu.VMEM((4 * ZN * HALF, TILE), jnp.float32)],
        compiler_params=pltpu.CompilerParams(vmem_limit_bytes=8 * MIB),
        name="by_rows",
    )(*pieces)


def join_kernel(spots, *refs):
    out_ref, sems = refs[-2], refs[-1]
    core, at0, at1 = spot()
    copies = []
    for i, (other, part, step) in enumerate(spots):
        half, at = (1 - core, at0) if other else (core, at1)
        copies.append(pltpu.make_async_copy(refs[i], out_ref.at[half, part, :, (at + 4 - step) % 4], sems.at[i]))
    for copy in copies:
        copy.start()
    for copy in copies:
        copy.wait()


def join(spots, pieces, out=None):
    n = len(spots)
    more = [] if out is None else [out]
    size = n * PART * 32 * TILE * 2
    return pl.pallas_call(
        functools.partial(join_kernel, spots),
        out_shape=jax.ShapeDtypeStruct((2, 2, PART, 4, 32, TILE), jnp.bfloat16),
        in_specs=[pl.BlockSpec(memory_space=pltpu.VMEM)] * n + [pl.BlockSpec(memory_space=pltpu.HBM)] * len(more),
        out_specs=pl.BlockSpec(memory_space=pltpu.HBM),
        scratch_shapes=[pltpu.SemaphoreType.DMA((n,))],
        input_output_aliases={} if out is None else {n: 0},
        compiler_params=pltpu.CompilerParams(vmem_limit_bytes=2 * MIB),
        cost_estimate=pl.CostEstimate(flops=0, bytes_accessed=2 * size, transcendentals=0),
        name="join",
    )(*pieces, *more)


def local(activations, cotangent, kept_tiles, kept_counts, chosen):
    me = lax.axis_index("dp")
    core = me % CN
    sent = own_tiles(kept_tiles.T, activations, cotangent)
    live = jnp.arange(KEPT, dtype=jnp.int32)[None, :] < kept_counts[:, None]
    ids = jnp.where(live, kept_tiles, -1).reshape(ZN, YN, XN, CN, KEPT)
    ids = lax.dynamic_index_in_dim(ids, core, 3, keepdims=False)
    ids = ids.transpose(1, 0, 2, 3).reshape(CHIPS * KEPT)
    got = lax.all_to_all(sent, "dp", 0, 0, axis_index_groups=CHIP_GROUPS, tiled=True)

    match = (chosen[:, None] == ids[None, :]).astype(jnp.float32)
    part = jnp.dot(match, got.reshape(CHIPS * KEPT, TILE), precision=lax.Precision.HIGHEST)
    part = part.reshape(CN, HALF, TILE)
    mine = lax.dynamic_index_in_dim(part, core, 0, keepdims=False)
    theirs = lax.dynamic_index_in_dim(part, 1 - core, 0, keepdims=False)
    row = (mine + lax.ppermute(theirs, "dp", SWAP)).astype(jnp.bfloat16)

    rows = lax.all_to_all(
        jnp.broadcast_to(row[None], (ZN, HALF, TILE)), "dp", 0, 0, axis_index_groups=Z_GROUPS, tiled=True
    )
    def swap(name, blocks):
        with jax.named_scope(name):
            return [lax.ppermute(b, "dp", SWAP) for b in blocks]

    def send(name, block, step):
        with jax.named_scope(name):
            return lax.ppermute(block, "dp", ring(step, 1))

    def both(steps):
        n = len(steps)
        return tuple((o, i * 2 // n, steps[i]) for o in range(2) for i in range(n))

    with jax.named_scope("s2"):
        pieces = [rows] + [lax.ppermute(rows, "dp", ring(s, 0)) for s in STEPS[1:]]
    a0, b0 = by_rows(pieces)
    a1 = send("a1", a0, 1)
    b3 = send("b3", b0, 3)
    b1 = send("b1", b0, 1)
    a3 = send("a3", a0, 3)
    own = swap("own", [a0, b0])
    out = join(both((0, 0)), [a0, b0] + own)
    a1, b3, out = lax.optimization_barrier((a1, b3, out))
    a2 = send("a2", a1, 1)
    b2 = send("b2", b3, 3)
    near = [a1, a3, b1, b3]
    out = join(both((1, 3, 1, 3)), near + swap("near", near), out)
    out = join(both((2, 2)), [a2, b2] + swap("far", [a2, b2]), out)
    return out.reshape(N_DP, TILE, TILE)


def solution(mesh):
    return jax.shard_map(
        local,
        mesh=mesh,
        in_specs=(P("dp", None), P("dp", None), P(), P(), P()),
        out_specs=P(),
        check_vma=False,
    )
```

```python
import functools

import jax
import jax.numpy as jnp
import numpy as np
from jax import lax
from jax.experimental import pallas as pl
from jax.experimental.pallas import tpu as pltpu
from jax.sharding import PartitionSpec as P

TILE = 128
KEPT = 8
N_DP = 256
COLS = 16
ZN, YN, XN, CN = 8, 4, 4, 2
CHIPS = 128
HALF = 128
HALF_TILES = 512
REGION = 4
MIB = 1024 * 1024
PART = 64
STEPS = (0, 2, 1, 3)


def dev(z, y, x, c):
    return ((z * YN + y) * XN + x) * CN + c


DEVS = [(z, y, x, c) for z in range(ZN) for y in range(YN) for x in range(XN) for c in range(CN)]
CHIP_GROUPS = [[dev(z, y, x, c) for y in range(YN) for z in range(ZN) for x in range(XN)] for c in range(CN)]
Z_GROUPS = [[dev(z, y, x, c) for z in range(ZN)] for y in range(YN) for x in range(XN) for c in range(CN)]
SWAP = [(d, d ^ 1) for d in range(N_DP)]


def ring(step, turn):
    pairs = []
    for z, y, x, c in DEVS:
        if (c + turn) % 2 == 0:
            pairs.append((dev(z, y, x, c), dev(z, (y + step) % YN, x, c)))
        else:
            pairs.append((dev(z, y, x, c), dev(z, y, (x + step) % XN, c)))
    return pairs


def spot():
    me = lax.axis_index("dp")
    core = me % CN
    x = (me // CN) % XN
    y = (me // (CN * XN)) % YN
    return core, jnp.where(core == 0, y, x), jnp.where(core == 0, x, y)


def tiles_kernel(kept_ref, act_ref, cot_ref, out_ref, lefts, rights, stage, sems):
    me = lax.axis_index("dp")
    for k in range(KEPT):
        tile = kept_ref[k, me]
        row = pl.multiple_of((tile // COLS) * TILE, TILE)
        col = pl.multiple_of((tile % COLS) * TILE, TILE)
        pltpu.make_async_copy(act_ref.at[:, pl.ds(row, TILE)], lefts.at[k], sems.at[0]).start()
        pltpu.make_async_copy(cot_ref.at[:, pl.ds(col, TILE)], rights.at[k], sems.at[1]).start()
    pltpu.make_async_copy(lefts, lefts, sems.at[0]).wait()
    pltpu.make_async_copy(rights, rights, sems.at[1]).wait()
    for k in range(KEPT):
        half = kept_ref[k, me] // HALF_TILES
        tile = lax.dot_general(
            lefts[k], rights[k], (((0,), (0,)), ((), ())), preferred_element_type=jnp.float32
        )
        for p in range(4):
            for q in range(4):
                there = jnp.where(half == 0, p * 32 + q * 8, q * 32 + p * 8) + k * TILE
                here = p * 32 + q * 8
                stage[pl.ds(pl.multiple_of(there, 8), 8), :] = tile[here:here + 8, :]
    for i, (y, z, x) in enumerate(np.ndindex(YN, ZN, XN)):
        out_ref[i] = stage[pl.ds(x * 32 + y * 8 + z, KEPT, stride=TILE), :]


def own_tiles(kept, activations, cotangent):
    return pl.pallas_call(
        tiles_kernel,
        out_shape=jax.ShapeDtypeStruct((CHIPS, KEPT, TILE), jnp.float32),
        in_specs=[
            pl.BlockSpec(memory_space=pltpu.SMEM),
            pl.BlockSpec(memory_space=pltpu.HBM),
            pl.BlockSpec(memory_space=pltpu.HBM),
        ],
        out_specs=pl.BlockSpec(memory_space=pltpu.VMEM),
        scratch_shapes=[
            pltpu.VMEM((KEPT, TILE, TILE), jnp.bfloat16),
            pltpu.VMEM((KEPT, TILE, TILE), jnp.bfloat16),
            pltpu.VMEM((KEPT * TILE, TILE), jnp.float32),
            pltpu.SemaphoreType.DMA((2,)),
        ],
        compiler_params=pltpu.CompilerParams(vmem_limit_bytes=62 * MIB),
        name="own_tiles",
    )(kept, activations, cotangent)


def sum_kernel(region_ref, got_ref, mine_ref, theirs_ref):
    core = lax.axis_index("dp") % CN
    rest = got_ref[...]
    parts = []
    for _ in range(3):
        parts.append(rest.astype(jnp.bfloat16))
        rest = rest - parts[-1].astype(jnp.float32)
    for ref, half in ((theirs_ref, 1 - core), (mine_ref, core)):
        tiles = lax.broadcasted_iota(jnp.int32, (HALF, CHIPS * KEPT), 0) + half * HALF
        match = (tiles == region_ref[...]).astype(jnp.float32).astype(jnp.bfloat16)
        sums = [jnp.dot(match, part, preferred_element_type=jnp.float32) for part in parts]
        ref[...] = (sums[2] + sums[1]) + sums[0]


def sum_tiles(region, got):
    return pl.pallas_call(
        sum_kernel,
        out_shape=[jax.ShapeDtypeStruct((HALF, TILE), jnp.float32)] * 2,
        in_specs=[pl.BlockSpec(memory_space=pltpu.VMEM)] * 2,
        out_specs=[pl.BlockSpec(memory_space=pltpu.VMEM)] * 2,
        compiler_params=pltpu.CompilerParams(vmem_limit_bytes=16 * MIB),
        name="sum_tiles",
    )(region, got)


def rows_kernel(p0, p1, p2, p3, a_ref, b_ref, wide):
    at = spot()[1]
    for step, piece in zip(STEPS, (p0, p1, p2, p3)):
        start = pl.multiple_of((at + 4 - step) % 4 * ZN * HALF, ZN * HALF)
        wide[pl.ds(start, ZN * HALF), :] = piece[...].astype(jnp.float32).reshape(ZN * HALF, TILE)

    for part, out_ref in enumerate((a_ref, b_ref)):
        def body(t, carry):
            rows = [wide[pl.ds(q * ZN * HALF + part * PART + t, ZN, stride=HALF), :] for q in range(4)]
            out_ref[t] = jnp.concatenate(rows, axis=0).astype(jnp.bfloat16)
            return carry

        lax.fori_loop(0, PART, body, 0, unroll=8)


def by_rows(pieces):
    return pl.pallas_call(
        rows_kernel,
        out_shape=[jax.ShapeDtypeStruct((PART, 4 * ZN, TILE), jnp.bfloat16)] * 2,
        in_specs=[pl.BlockSpec(memory_space=pltpu.VMEM)] * 4,
        out_specs=[pl.BlockSpec(memory_space=pltpu.VMEM)] * 2,
        scratch_shapes=[pltpu.VMEM((4 * ZN * HALF, TILE), jnp.float32)],
        compiler_params=pltpu.CompilerParams(vmem_limit_bytes=8 * MIB),
        name="by_rows",
    )(*pieces)


def join_kernel(spots, *refs):
    out_ref, sems = refs[-2], refs[-1]
    core, at0, at1 = spot()
    copies = []
    for i, (other, part, step) in enumerate(spots):
        half, at = (1 - core, at0) if other else (core, at1)
        copies.append(pltpu.make_async_copy(refs[i], out_ref.at[half, part, :, (at + 4 - step) % 4], sems.at[i]))
    for copy in copies:
        copy.start()
    for copy in copies:
        copy.wait()


def join(spots, pieces, out=None):
    n = len(spots)
    more = [] if out is None else [out]
    size = n * PART * 32 * TILE * 2
    return pl.pallas_call(
        functools.partial(join_kernel, spots),
        out_shape=jax.ShapeDtypeStruct((2, 2, PART, 4, 32, TILE), jnp.bfloat16),
        in_specs=[pl.BlockSpec(memory_space=pltpu.VMEM)] * n + [pl.BlockSpec(memory_space=pltpu.HBM)] * len(more),
        out_specs=pl.BlockSpec(memory_space=pltpu.HBM),
        scratch_shapes=[pltpu.SemaphoreType.DMA((n,))],
        input_output_aliases={} if out is None else {n: 0},
        compiler_params=pltpu.CompilerParams(vmem_limit_bytes=2 * MIB),
        cost_estimate=pl.CostEstimate(flops=0, bytes_accessed=2 * size, transcendentals=0),
        name="join",
    )(*pieces, *more)


def local(activations, cotangent, kept_tiles, kept_counts, chosen):
    me = lax.axis_index("dp")
    core = me % CN
    sent = own_tiles(kept_tiles.T, activations, cotangent)
    live = jnp.arange(KEPT, dtype=jnp.int32)[None, :] < kept_counts[:, None]
    hit = jnp.any(kept_tiles[:, :, None] == chosen[None, None, :], axis=-1)
    region = jnp.where(live & hit, kept_tiles // REGION, -1).reshape(ZN, YN, XN, CN, KEPT)
    region = lax.dynamic_index_in_dim(region, core, 3, keepdims=False)
    region = region.transpose(1, 0, 2, 3).reshape(1, CHIPS * KEPT)
    got = lax.all_to_all(sent, "dp", 0, 0, axis_index_groups=CHIP_GROUPS, tiled=True)
    mine, theirs = sum_tiles(region, got.reshape(CHIPS * KEPT, TILE))
    row = (mine + lax.ppermute(theirs, "dp", SWAP)).astype(jnp.bfloat16)

    rows = lax.all_to_all(
        jnp.broadcast_to(row[None], (ZN, HALF, TILE)), "dp", 0, 0, axis_index_groups=Z_GROUPS, tiled=True
    )
    def swap(name, blocks):
        with jax.named_scope(name):
            return [lax.ppermute(b, "dp", SWAP) for b in blocks]

    def send(name, block, step):
        with jax.named_scope(name):
            return lax.ppermute(block, "dp", ring(step, 1))

    def both(steps):
        n = len(steps)
        return tuple((o, i * 2 // n, steps[i]) for o in range(2) for i in range(n))

    with jax.named_scope("s2"):
        pieces = [rows] + [lax.ppermute(rows, "dp", ring(s, 0)) for s in STEPS[1:]]
    a0, b0 = by_rows(pieces)
    a1 = send("a1", a0, 1)
    b3 = send("b3", b0, 3)
    b1 = send("b1", b0, 1)
    a3 = send("a3", a0, 3)
    own = swap("own", [a0, b0])
    out = join(both((0, 0)), [a0, b0] + own)
    a1, b3, out = lax.optimization_barrier((a1, b3, out))
    a2 = send("a2", a1, 1)
    b2 = send("b2", b3, 3)
    near = [a1, a3, b1, b3]
    out = join(both((1, 3, 1, 3)), near + swap("near", near), out)
    out = join(both((2, 2)), [a2, b2] + swap("far", [a2, b2]), out)
    return out.reshape(N_DP, TILE, TILE)


def solution(mesh):
    return jax.shard_map(
        local,
        mesh=mesh,
        in_specs=(P("dp", None), P("dp", None), P(), P(), P()),
        out_specs=P(),
        check_vma=False,
    )
```

```python
import functools

import jax
import jax.numpy as jnp
import numpy as np
from jax import lax
from jax.experimental import pallas as pl
from jax.experimental.pallas import tpu as pltpu
from jax.sharding import PartitionSpec as P

TILE = 128
KEPT = 8
N_DP = 256
COLS = 16
ZN, YN, XN, CN = 8, 4, 4, 2
CHIPS = 128
HALF = 128
HALF_TILES = 512
REGION = 4
MIB = 1024 * 1024
PART = 64
STEPS = (0, 2, 1, 3)


def dev(z, y, x, c):
    return ((z * YN + y) * XN + x) * CN + c


DEVS = [(z, y, x, c) for z in range(ZN) for y in range(YN) for x in range(XN) for c in range(CN)]
CHIP_GROUPS = [[dev(z, y, x, c) for y in range(YN) for z in range(ZN) for x in range(XN)] for c in range(CN)]
Z_GROUPS = [[dev(z, y, x, c) for z in range(ZN)] for y in range(YN) for x in range(XN) for c in range(CN)]
SWAP = [(d, d ^ 1) for d in range(N_DP)]


def ring(step, turn):
    pairs = []
    for z, y, x, c in DEVS:
        if (c + turn) % 2 == 0:
            pairs.append((dev(z, y, x, c), dev(z, (y + step) % YN, x, c)))
        else:
            pairs.append((dev(z, y, x, c), dev(z, y, (x + step) % XN, c)))
    return pairs


def spot():
    me = lax.axis_index("dp")
    core = me % CN
    x = (me // CN) % XN
    y = (me // (CN * XN)) % YN
    return core, jnp.where(core == 0, y, x), jnp.where(core == 0, x, y)


def tiles_kernel(kept_ref, act_ref, cot_ref, out_ref, lefts, rights, stage, sems):
    me = lax.axis_index("dp")
    whole = pltpu.make_async_copy(cot_ref, rights, sems.at[1])
    whole.start()
    for k in range(KEPT):
        row = pl.multiple_of((kept_ref[k, me] // COLS) * TILE, TILE)
        pltpu.make_async_copy(act_ref.at[:, pl.ds(row, TILE)], lefts.at[k], sems.at[0]).start()
    whole.wait()
    pltpu.make_async_copy(lefts, lefts, sems.at[0]).wait()
    for k in range(KEPT):
        half = kept_ref[k, me] // HALF_TILES
        col = pl.multiple_of((kept_ref[k, me] % COLS) * TILE, TILE)
        tile = lax.dot_general(
            lefts[k], rights[:, pl.ds(col, TILE)], (((0,), (0,)), ((), ())), preferred_element_type=jnp.float32
        )
        for p in range(4):
            for q in range(4):
                there = jnp.where(half == 0, p * 32 + q * 8, q * 32 + p * 8) + k * TILE
                here = p * 32 + q * 8
                stage[pl.ds(pl.multiple_of(there, 8), 8), :] = tile[here:here + 8, :]
    for i, (y, z, x) in enumerate(np.ndindex(YN, ZN, XN)):
        out_ref[i] = stage[pl.ds(x * 32 + y * 8 + z, KEPT, stride=TILE), :]


def own_tiles(kept, activations, cotangent):
    return pl.pallas_call(
        tiles_kernel,
        out_shape=jax.ShapeDtypeStruct((CHIPS, KEPT, TILE), jnp.float32),
        in_specs=[
            pl.BlockSpec(memory_space=pltpu.SMEM),
            pl.BlockSpec(memory_space=pltpu.HBM),
            pl.BlockSpec(memory_space=pltpu.HBM),
        ],
        out_specs=pl.BlockSpec(memory_space=pltpu.VMEM),
        scratch_shapes=[
            pltpu.VMEM((KEPT, TILE, TILE), jnp.bfloat16),
            pltpu.VMEM((TILE, COLS * TILE), jnp.bfloat16),
            pltpu.VMEM((KEPT * TILE, TILE), jnp.float32),
            pltpu.SemaphoreType.DMA((2,)),
        ],
        compiler_params=pltpu.CompilerParams(vmem_limit_bytes=62 * MIB),
        name="own_tiles",
    )(kept, activations, cotangent)


def sum_kernel(region_ref, got_ref, mine_ref, theirs_ref):
    core = lax.axis_index("dp") % CN
    rest = got_ref[...]
    parts = []
    for _ in range(3):
        parts.append(rest.astype(jnp.bfloat16))
        rest = rest - parts[-1].astype(jnp.float32)
    for ref, half in ((theirs_ref, 1 - core), (mine_ref, core)):
        tiles = lax.broadcasted_iota(jnp.int32, (HALF, CHIPS * KEPT), 0) + half * HALF
        match = (tiles == region_ref[...]).astype(jnp.float32).astype(jnp.bfloat16)
        sums = [jnp.dot(match, part, preferred_element_type=jnp.float32) for part in parts]
        ref[...] = (sums[2] + sums[1]) + sums[0]


def sum_tiles(region, got):
    return pl.pallas_call(
        sum_kernel,
        out_shape=[jax.ShapeDtypeStruct((HALF, TILE), jnp.float32)] * 2,
        in_specs=[pl.BlockSpec(memory_space=pltpu.VMEM)] * 2,
        out_specs=[pl.BlockSpec(memory_space=pltpu.VMEM)] * 2,
        compiler_params=pltpu.CompilerParams(vmem_limit_bytes=16 * MIB),
        name="sum_tiles",
    )(region, got)


def rows_kernel(p0, p1, p2, p3, a_ref, b_ref, wide):
    at = spot()[1]
    for step, piece in zip(STEPS, (p0, p1, p2, p3)):
        start = pl.multiple_of((at + 4 - step) % 4 * ZN * HALF, ZN * HALF)
        wide[pl.ds(start, ZN * HALF), :] = piece[...].astype(jnp.float32).reshape(ZN * HALF, TILE)

    for part, out_ref in enumerate((a_ref, b_ref)):
        def body(t, carry):
            rows = [wide[pl.ds(q * ZN * HALF + part * PART + t, ZN, stride=HALF), :] for q in range(4)]
            out_ref[t] = jnp.concatenate(rows, axis=0).astype(jnp.bfloat16)
            return carry

        lax.fori_loop(0, PART, body, 0, unroll=32)


def by_rows(pieces):
    return pl.pallas_call(
        rows_kernel,
        out_shape=[jax.ShapeDtypeStruct((PART, 4 * ZN, TILE), jnp.bfloat16)] * 2,
        in_specs=[pl.BlockSpec(memory_space=pltpu.VMEM)] * 4,
        out_specs=[pl.BlockSpec(memory_space=pltpu.VMEM)] * 2,
        scratch_shapes=[pltpu.VMEM((4 * ZN * HALF, TILE), jnp.float32)],
        compiler_params=pltpu.CompilerParams(vmem_limit_bytes=8 * MIB),
        name="by_rows",
    )(*pieces)


def join_kernel(spots, *refs):
    out_ref, sems = refs[-2], refs[-1]
    core, at0, at1 = spot()
    copies = []
    for i, (other, part, step) in enumerate(spots):
        half, at = (1 - core, at0) if other else (core, at1)
        copies.append(pltpu.make_async_copy(refs[i], out_ref.at[half, part, :, (at + 4 - step) % 4], sems.at[i]))
    for copy in copies:
        copy.start()
    for copy in copies:
        copy.wait()


def join(spots, pieces, out=None):
    n = len(spots)
    more = [] if out is None else [out]
    size = n * PART * 32 * TILE * 2
    return pl.pallas_call(
        functools.partial(join_kernel, spots),
        out_shape=jax.ShapeDtypeStruct((2, 2, PART, 4, 32, TILE), jnp.bfloat16),
        in_specs=[pl.BlockSpec(memory_space=pltpu.VMEM)] * n + [pl.BlockSpec(memory_space=pltpu.HBM)] * len(more),
        out_specs=pl.BlockSpec(memory_space=pltpu.HBM),
        scratch_shapes=[pltpu.SemaphoreType.DMA((n,))],
        input_output_aliases={} if out is None else {n: 0},
        compiler_params=pltpu.CompilerParams(vmem_limit_bytes=2 * MIB),
        cost_estimate=pl.CostEstimate(flops=0, bytes_accessed=2 * size, transcendentals=0),
        name="join",
    )(*pieces, *more)


def local(activations, cotangent, kept_tiles, kept_counts, chosen):
    me = lax.axis_index("dp")
    core = me % CN
    sent = own_tiles(kept_tiles.T, activations, cotangent)
    live = jnp.arange(KEPT, dtype=jnp.int32)[None, :] < kept_counts[:, None]
    hit = jnp.any(kept_tiles[:, :, None] == chosen[None, None, :], axis=-1)
    region = jnp.where(live & hit, kept_tiles // REGION, -1).reshape(ZN, YN, XN, CN, KEPT)
    region = lax.dynamic_index_in_dim(region, core, 3, keepdims=False)
    region = region.transpose(1, 0, 2, 3).reshape(1, CHIPS * KEPT)
    got = lax.all_to_all(sent, "dp", 0, 0, axis_index_groups=CHIP_GROUPS, tiled=True)
    mine, theirs = sum_tiles(region, got.reshape(CHIPS * KEPT, TILE))
    row = (mine + lax.ppermute(theirs, "dp", SWAP)).astype(jnp.bfloat16)

    rows = lax.all_to_all(
        jnp.broadcast_to(row[None], (ZN, HALF, TILE)), "dp", 0, 0, axis_index_groups=Z_GROUPS, tiled=True
    )
    def swap(name, blocks):
        with jax.named_scope(name):
            return [lax.ppermute(b, "dp", SWAP) for b in blocks]

    def send(name, block, step):
        with jax.named_scope(name):
            return lax.ppermute(block, "dp", ring(step, 1))

    def both(steps):
        n = len(steps)
        return tuple((o, i * 2 // n, steps[i]) for o in range(2) for i in range(n))

    with jax.named_scope("s2"):
        pieces = [rows] + [lax.ppermute(rows, "dp", ring(s, 0)) for s in STEPS[1:]]
    a0, b0 = by_rows(pieces)
    a1 = send("a1", a0, 1)
    b3 = send("b3", b0, 3)
    b1 = send("b1", b0, 1)
    a3 = send("a3", a0, 3)
    own = swap("own", [a0, b0])
    out = join(both((0, 0)), [a0, b0] + own)
    a1, b3, out = lax.optimization_barrier((a1, b3, out))
    a2 = send("a2", a1, 1)
    b2 = send("b2", b3, 3)
    near = [a1, a3, b1, b3]
    out = join(both((1, 3, 1, 3)), near + swap("near", near), out)
    out = join(both((2, 2)), [a2, b2] + swap("far", [a2, b2]), out)
    return out.reshape(N_DP, TILE, TILE)


def solution(mesh):
    return jax.shard_map(
        local,
        mesh=mesh,
        in_specs=(P("dp", None), P("dp", None), P(), P(), P()),
        out_specs=P(),
        check_vma=False,
    )
```

```python
import functools

import jax
import jax.numpy as jnp
import numpy as np
from jax import lax
from jax.experimental import pallas as pl
from jax.experimental.pallas import tpu as pltpu
from jax.sharding import PartitionSpec as P

TILE = 128
KEPT = 8
N_DP = 256
COLS = 16
ZN, YN, XN, CN = 8, 4, 4, 2
CHIPS = 128
HALF = 128
HALF_TILES = 512
REGION = 4
MIB = 1024 * 1024
PART = 64
STEPS = (0, 2, 1, 3)


def dev(z, y, x, c):
    return ((z * YN + y) * XN + x) * CN + c


DEVS = [(z, y, x, c) for z in range(ZN) for y in range(YN) for x in range(XN) for c in range(CN)]
ORDER = [37 * i % CHIPS for i in range(CHIPS)]
CHIP_GROUPS = [[chip * CN + c for chip in ORDER] for c in range(CN)]
Z_GROUPS = [[dev(z, y, x, c) for z in range(ZN)] for y in range(YN) for x in range(XN) for c in range(CN)]
SWAP = [(d, d ^ 1) for d in range(N_DP)]


def ring(step, turn):
    pairs = []
    for z, y, x, c in DEVS:
        if (c + turn) % 2 == 0:
            pairs.append((dev(z, y, x, c), dev(z, (y + step) % YN, x, c)))
        else:
            pairs.append((dev(z, y, x, c), dev(z, y, (x + step) % XN, c)))
    return pairs


def spot():
    me = lax.axis_index("dp")
    core = me % CN
    x = (me // CN) % XN
    y = (me // (CN * XN)) % YN
    return core, jnp.where(core == 0, y, x), jnp.where(core == 0, x, y)


def tiles_kernel(kept_ref, act_ref, cot_ref, out_ref, lefts, rights, stage, sems):
    me = lax.axis_index("dp")
    for k in range(KEPT):
        tile = kept_ref[k, me]
        row = pl.multiple_of((tile // COLS) * TILE, TILE)
        col = pl.multiple_of((tile % COLS) * TILE, TILE)
        pltpu.make_async_copy(act_ref.at[:, pl.ds(row, TILE)], lefts.at[k], sems.at[0]).start()
        pltpu.make_async_copy(cot_ref.at[:, pl.ds(col, TILE)], rights.at[k], sems.at[1]).start()
    pltpu.make_async_copy(lefts, lefts, sems.at[0]).wait()
    pltpu.make_async_copy(rights, rights, sems.at[1]).wait()
    for k in range(KEPT):
        half = kept_ref[k, me] // HALF_TILES
        tile = lax.dot_general(
            lefts[k], rights[k], (((0,), (0,)), ((), ())), preferred_element_type=jnp.float32
        )
        for p in range(4):
            for q in range(4):
                there = jnp.where(half == 0, p * 32 + q * 8, q * 32 + p * 8) + k * TILE
                here = p * 32 + q * 8
                stage[pl.ds(pl.multiple_of(there, 8), 8), :] = tile[here:here + 8, :]
    for i, chip in enumerate(ORDER):
        z, y, x = chip // 16, (chip // 4) % 4, chip % 4
        out_ref[i] = stage[pl.ds(x * 32 + y * 8 + z, KEPT, stride=TILE), :]


def own_tiles(kept, activations, cotangent):
    return pl.pallas_call(
        tiles_kernel,
        out_shape=jax.ShapeDtypeStruct((CHIPS, KEPT, TILE), jnp.float32),
        in_specs=[
            pl.BlockSpec(memory_space=pltpu.SMEM),
            pl.BlockSpec(memory_space=pltpu.HBM),
            pl.BlockSpec(memory_space=pltpu.HBM),
        ],
        out_specs=pl.BlockSpec(memory_space=pltpu.VMEM),
        scratch_shapes=[
            pltpu.VMEM((KEPT, TILE, TILE), jnp.bfloat16),
            pltpu.VMEM((KEPT, TILE, TILE), jnp.bfloat16),
            pltpu.VMEM((KEPT * TILE, TILE), jnp.float32),
            pltpu.SemaphoreType.DMA((2,)),
        ],
        compiler_params=pltpu.CompilerParams(vmem_limit_bytes=62 * MIB),
        name="own_tiles",
    )(kept, activations, cotangent)


def sum_kernel(region_ref, got_ref, mine_ref, theirs_ref):
    core = lax.axis_index("dp") % CN
    rest = got_ref[...]
    parts = []
    for _ in range(3):
        parts.append(rest.astype(jnp.bfloat16))
        rest = rest - parts[-1].astype(jnp.float32)
    for ref, half in ((theirs_ref, 1 - core), (mine_ref, core)):
        tiles = lax.broadcasted_iota(jnp.int32, (HALF, CHIPS * KEPT), 0) + half * HALF
        match = (tiles == region_ref[...]).astype(jnp.float32).astype(jnp.bfloat16)
        sums = [jnp.dot(match, part, preferred_element_type=jnp.float32) for part in parts]
        ref[...] = (sums[2] + sums[1]) + sums[0]


def sum_tiles(region, got):
    return pl.pallas_call(
        sum_kernel,
        out_shape=[jax.ShapeDtypeStruct((HALF, TILE), jnp.float32)] * 2,
        in_specs=[pl.BlockSpec(memory_space=pltpu.VMEM)] * 2,
        out_specs=[pl.BlockSpec(memory_space=pltpu.VMEM)] * 2,
        compiler_params=pltpu.CompilerParams(vmem_limit_bytes=16 * MIB),
        name="sum_tiles",
    )(region, got)


def rows_kernel(p0, p1, p2, p3, a_ref, b_ref, wide):
    at = spot()[1]
    for step, piece in zip(STEPS, (p0, p1, p2, p3)):
        start = pl.multiple_of((at + 4 - step) % 4 * ZN * HALF, ZN * HALF)
        wide[pl.ds(start, ZN * HALF), :] = piece[...].astype(jnp.float32).reshape(ZN * HALF, TILE)

    for part, out_ref in enumerate((a_ref, b_ref)):
        def body(t, carry):
            rows = [wide[pl.ds(q * ZN * HALF + part * PART + t, ZN, stride=HALF), :] for q in range(4)]
            out_ref[t] = jnp.concatenate(rows, axis=0).astype(jnp.bfloat16)
            return carry

        lax.fori_loop(0, PART, body, 0, unroll=8)


def by_rows(pieces):
    return pl.pallas_call(
        rows_kernel,
        out_shape=[jax.ShapeDtypeStruct((PART, 4 * ZN, TILE), jnp.bfloat16)] * 2,
        in_specs=[pl.BlockSpec(memory_space=pltpu.VMEM)] * 4,
        out_specs=[pl.BlockSpec(memory_space=pltpu.VMEM)] * 2,
        scratch_shapes=[pltpu.VMEM((4 * ZN * HALF, TILE), jnp.float32)],
        compiler_params=pltpu.CompilerParams(vmem_limit_bytes=8 * MIB),
        name="by_rows",
    )(*pieces)


def join_kernel(spots, *refs):
    out_ref, sems = refs[-2], refs[-1]
    core, at0, at1 = spot()
    copies = []
    for i, (other, part, step) in enumerate(spots):
        half, at = (1 - core, at0) if other else (core, at1)
        copies.append(pltpu.make_async_copy(refs[i], out_ref.at[half, part, :, (at + 4 - step) % 4], sems.at[i]))
    for copy in copies:
        copy.start()
    for copy in copies:
        copy.wait()


def join(spots, pieces, out=None):
    n = len(spots)
    more = [] if out is None else [out]
    size = n * PART * 32 * TILE * 2
    return pl.pallas_call(
        functools.partial(join_kernel, spots),
        out_shape=jax.ShapeDtypeStruct((2, 2, PART, 4, 32, TILE), jnp.bfloat16),
        in_specs=[pl.BlockSpec(memory_space=pltpu.VMEM)] * n + [pl.BlockSpec(memory_space=pltpu.HBM)] * len(more),
        out_specs=pl.BlockSpec(memory_space=pltpu.HBM),
        scratch_shapes=[pltpu.SemaphoreType.DMA((n,))],
        input_output_aliases={} if out is None else {n: 0},
        compiler_params=pltpu.CompilerParams(vmem_limit_bytes=2 * MIB),
        cost_estimate=pl.CostEstimate(flops=0, bytes_accessed=2 * size, transcendentals=0),
        name="join",
    )(*pieces, *more)


def local(activations, cotangent, kept_tiles, kept_counts, chosen):
    me = lax.axis_index("dp")
    core = me % CN
    sent = own_tiles(kept_tiles.T, activations, cotangent)
    live = jnp.arange(KEPT, dtype=jnp.int32)[None, :] < kept_counts[:, None]
    hit = jnp.any(kept_tiles[:, :, None] == chosen[None, None, :], axis=-1)
    region = jnp.where(live & hit, kept_tiles // REGION, -1).reshape(CHIPS, CN, KEPT)
    region = lax.dynamic_index_in_dim(region, core, 1, keepdims=False)
    region = region[np.array(ORDER)].reshape(1, CHIPS * KEPT)
    got = lax.all_to_all(sent, "dp", 0, 0, axis_index_groups=CHIP_GROUPS, tiled=True)
    mine, theirs = sum_tiles(region, got.reshape(CHIPS * KEPT, TILE))
    row = (mine + lax.ppermute(theirs, "dp", SWAP)).astype(jnp.bfloat16)

    rows = lax.all_to_all(
        jnp.broadcast_to(row[None], (ZN, HALF, TILE)), "dp", 0, 0, axis_index_groups=Z_GROUPS, tiled=True
    )
    def swap(name, blocks):
        with jax.named_scope(name):
            return [lax.ppermute(b, "dp", SWAP) for b in blocks]

    def send(name, block, step):
        with jax.named_scope(name):
            return lax.ppermute(block, "dp", ring(step, 1))

    def both(steps):
        n = len(steps)
        return tuple((o, i * 2 // n, steps[i]) for o in range(2) for i in range(n))

    with jax.named_scope("s2"):
        pieces = [rows] + [lax.ppermute(rows, "dp", ring(s, 0)) for s in STEPS[1:]]
    a0, b0 = by_rows(pieces)
    a1 = send("a1", a0, 1)
    b3 = send("b3", b0, 3)
    b1 = send("b1", b0, 1)
    a3 = send("a3", a0, 3)
    own = swap("own", [a0, b0])
    out = join(both((0, 0)), [a0, b0] + own)
    a1, b3, out = lax.optimization_barrier((a1, b3, out))
    a2 = send("a2", a1, 1)
    b2 = send("b2", b3, 3)
    near = [a1, a3, b1, b3]
    out = join(both((1, 3, 1, 3)), near + swap("near", near), out)
    out = join(both((2, 2)), [a2, b2] + swap("far", [a2, b2]), out)
    return out.reshape(N_DP, TILE, TILE)


def solution(mesh):
    return jax.shard_map(
        local,
        mesh=mesh,
        in_specs=(P("dp", None), P("dp", None), P(), P(), P()),
        out_specs=P(),
        check_vma=False,
    )
```
